256 devices in a mesh: dp: 8 (over z), ctx: 8 (over x_lo, y), tensor: 4 (over x_hi, core).
Axes of the slice: x: 4 (x_hi: 2, x_lo: 2; x = x_hi * 2 + x_lo), y: 4, z: 8, core: 2. Of those that a mesh axis runs over, the one named last changes fastest.
Arguments:
- tokens: bfloat16 [8192, 8192], P(('dp', 'ctx'), 'tensor'), may hold values from -6 to 6
- queries: bfloat16 [8192, 4096], P(('dp', 'ctx'), 'tensor'), may hold values from -110 to 110
- values: bfloat16 [8192, 512], P(('dp', 'ctx'), 'tensor'), may hold values from -6 to 6
- out_grad: bfloat16 [8192, 4096], P(('dp', 'ctx'), 'tensor'), may hold values from -6 to 6
- key_weight: bfloat16 [512, 8192], P(None, 'tensor'), may hold values from -0.0625 to 0.0625
- plan: int32 [64, 32], replicated, may hold values from 0 to 63, as said below
- lengths: int32 [8, 16], replicated, may hold values from 0 to 1024, as said below
Outputs:
- attended: bfloat16 [8192, 4096], P(('dp', 'ctx'), 'tensor')
- query_grad: bfloat16 [8192, 4096], P(('dp', 'ctx'), 'tensor')
- value_grad: bfloat16 [8192, 512], P(('dp', 'ctx'), 'tensor')
- feature_grad: bfloat16 [8192, 8192], P(('dp', 'ctx'), 'tensor')
- key_weight_grad: float32 [512, 8192], P(('dp', 'ctx'), 'tensor')
The draws below stay inside these ranges and needn't reach their ends.
Inputs may be any that keep to these rules, and one draw needn't show every extreme that they name: `plan`: no row names a loader twice, and every loader is named exactly 32 times. `lengths`: each row sums to 1024; exactly one row is a single sequence of 1024 followed by zeros; every other row holds 16 sequences of 1 or more tokens.
All inputs are finite; a program needn't handle non-finite values.
Results may differ from the reference program's by a relative error of at most 0.035.
The reference program's roundings to bfloat16 on the way (of `features`, `key_proj`, `keys`, `weights`, `dscore` and `key_grad`) count: a program that leaves them out, or rounds other values in their place, can miss the bound.
Values may be sent and summed in bfloat16 or wider, within the bound.
A program may use at most 64 MiB of HBM per device.

```python
import math
import jax
import jax.numpy as jnp
from jax import lax

D = 8192
QHEADS = 32
KVHEADS = 4
HEAD = 128
MAXSEQ = 16
LOADERS = 64
SLABS_DEV = 32
SLAB_ROWS = 4
GROUP = 1024
TOKENS = 8192
QW = 4096
KVW = 512
N_DP = 8


def draw_queries(key, part):
    key = jax.random.fold_in(key, 37)
    base_key = jax.random.fold_in(key, 0)
    result = jnp.clip(jax.random.normal(base_key, (TOKENS, QW), jnp.float32), -6.0, 6.0)
    return result.astype(jnp.bfloat16)


def draw_plan(key, part):
    key = jax.random.fold_in(key, 11)
    outer_key, inner_key, shift_key = jax.random.split(key, 3)
    outer = jax.random.permutation(outer_key, LOADERS)
    inner = jax.random.permutation(inner_key, LOADERS)
    shifts = jax.random.permutation(shift_key, LOADERS)[:SLABS_DEV]
    spots = (inner[:, None] + shifts[None, :]) % LOADERS
    return outer[spots].astype(jnp.int32)


def draw_lengths(key, part):
    key = jax.random.fold_in(key, 23)
    weight_key, group_key = jax.random.split(key)
    weights = jax.random.randint(weight_key, (N_DP, MAXSEQ), 1, 33)
    spare = GROUP - MAXSEQ
    shares = 1 + spare * weights // jnp.sum(weights, axis=1, keepdims=True)
    leading = shares[:, :-1]
    closing = GROUP - jnp.sum(leading, axis=1, keepdims=True)
    packed = jnp.concatenate([leading, closing], axis=1)
    single = jnp.concatenate([jnp.full((1, 1), GROUP, jnp.int32), jnp.zeros((1, MAXSEQ - 1), jnp.int32)], axis=1)
    chosen = jax.random.randint(group_key, (), 0, N_DP)
    is_single = jnp.arange(N_DP)[:, None] == chosen
    return jnp.where(is_single, single, packed).astype(jnp.int32)


def levels(key, dims, cuts, low, largest):
    def one(dim, parts):
        draws = jax.random.uniform(jax.random.fold_in(jax.random.fold_in(key, 6), dim), (parts,), jnp.float32, low / len(cuts), largest / len(cuts))
        return jnp.repeat(jnp.exp(draws), dims[dim] // parts).reshape((-1,) + (1,) * (len(dims) - dim - 1))

    factor_of = one(*cuts[0])
    for cut in cuts[1:]:
        factor_of = factor_of * one(*cut)
    return factor_of


def noise(rng, shape, width, reach, shards=(), held_as=jnp.bfloat16):
    entries = jax.random.normal(rng, shape, jnp.float32) * width
    if len(shards) > 0:
        entries = levels(rng, shape, shards, -0.22, 0.18) * entries
    return jnp.clip(entries, min=-reach, max=reach).astype(held_as)


def setup_inputs(seed: int = 0) -> dict:
    splits = jax.random.split(jax.random.key(seed), 8)
    return {
        "tokens": noise(splits[0], (TOKENS, D), 1.0, 6.0, ((0, 64), (1, 4))),
        "queries": draw_queries(jax.random.fold_in(splits[7], 71), 0),
        "values": noise(splits[2], (TOKENS, KVW), 1.0, 6.0, ((0, 64), (1, 4))),
        "out_grad": noise(splits[3], (TOKENS, QW), 1.0, 6.0, ((0, 64), (1, 4))),
        "key_weight": noise(splits[4], (KVW, D), D ** -0.5, 0.0625, ((1, 4),)),
        "plan": draw_plan(jax.random.fold_in(splits[7], 71), 0),
        "lengths": draw_lengths(jax.random.fold_in(splits[7], 71), 0),
    }


theta_base = 500000.0
masked_score = -1e30


def rotary_tables(offsets):
    half_dim = HEAD // 2
    exponent = jnp.arange(half_dim, dtype=jnp.float32) * (2.0 / HEAD)
    frequency = jnp.exp(-exponent * math.log(theta_base))
    angle = offsets.astype(jnp.float32)[:, None] * frequency[None, :]
    return jnp.cos(angle), jnp.sin(angle)


def rotate(inputs, cosine, sine):
    half_dim = HEAD // 2
    first_half = inputs[..., :half_dim]
    second_half = inputs[..., half_dim:]
    return jnp.concatenate([first_half * cosine - second_half * sine, second_half * cosine + first_half * sine], axis=-1)


def unrotate(grads, cosine, sine):
    half_dim = HEAD // 2
    first_half = grads[..., :half_dim]
    second_half = grads[..., half_dim:]
    return jnp.concatenate([first_half * cosine + second_half * sine, second_half * cosine - first_half * sine], axis=-1)


def reference(tokens, queries, values, out_grad, key_weight, plan, lengths):
    slab_total = LOADERS * SLABS_DEV
    destination = plan.reshape(slab_total).astype(jnp.int32)
    sender = (jnp.arange(slab_total, dtype=jnp.int32) // SLABS_DEV).astype(jnp.int32)
    order = jnp.argsort(destination * LOADERS + sender).astype(jnp.int32)
    inverse = jnp.argsort(order).astype(jnp.int32)

    def to_context(array):
        return array.reshape(slab_total, SLAB_ROWS, -1)[order].reshape(TOKENS, -1)

    def to_loader(array):
        return array.reshape(slab_total, SLAB_ROWS, -1)[inverse].reshape(TOKENS, -1)

    features = to_context(tokens)
    query_ctx = to_context(queries)
    value_ctx = to_context(values)
    grad_ctx = to_context(out_grad)
    key_proj = jnp.dot(features, key_weight.T, preferred_element_type=jnp.float32).astype(jnp.bfloat16)
    key_proj = lax.optimization_barrier(key_proj)
    position = jnp.arange(GROUP, dtype=jnp.int32)
    ends = jnp.cumsum(lengths, axis=1).astype(jnp.int32)
    per_group = QHEADS // KVHEADS
    scale = HEAD ** -0.5
    attended_groups, query_groups, value_groups, key_groups = [], [], [], []
    for group in range(N_DP):
        low = group * GROUP
        seq_start = jnp.sum(lengths[group][None, :] * (ends[group][None, :] <= position[:, None]).astype(jnp.int32), axis=1).astype(jnp.int32)
        cosine, sine = rotary_tables(position - seq_start)
        visible = (position[None, :] <= position[:, None]) & (position[None, :] >= seq_start[:, None])
        attended_heads, query_heads, value_heads, key_heads = [], [], [], []
        for head in range(KVHEADS):
            kv_low = head * HEAD
            q_low = head * per_group * HEAD
            raw_key = key_proj[low:low + GROUP, kv_low:kv_low + HEAD].astype(jnp.float32)
            keys = rotate(raw_key, cosine, sine).astype(jnp.bfloat16)
            key_float = keys.astype(jnp.float32)
            value_float = value_ctx[low:low + GROUP, kv_low:kv_low + HEAD].astype(jnp.float32)
            query_block = query_ctx[low:low + GROUP, q_low:q_low + per_group * HEAD].reshape(GROUP, per_group, HEAD).astype(jnp.float32)
            grad_block = grad_ctx[low:low + GROUP, q_low:q_low + per_group * HEAD].reshape(GROUP, per_group, HEAD).astype(jnp.float32)
            scores = jnp.einsum('qhd,kd->hqk', query_block, key_float) * scale
            scores = jnp.where(visible[None], scores, masked_score)
            highest = jnp.max(scores, axis=2)
            summed = jnp.sum(jnp.where(visible[None], jnp.exp(scores - highest[..., None]), 0.0), axis=2)
            log_total = highest + jnp.log(summed)
            prob = jnp.where(visible[None], jnp.exp(scores - log_total[..., None]), 0.0)
            weights = lax.optimization_barrier(prob.astype(jnp.bfloat16)).astype(jnp.float32)
            attended = jnp.einsum('hqk,kd->qhd', weights, value_float).astype(jnp.bfloat16)
            delta = jnp.sum(grad_block * attended.astype(jnp.float32), axis=2).T
            dprob = jnp.einsum('qhd,kd->hqk', grad_block, value_float)
            dscore = lax.optimization_barrier((prob * (dprob - delta[..., None])).astype(jnp.bfloat16)).astype(jnp.float32)
            query_grad = (jnp.einsum('hqk,kd->qhd', dscore, key_float) * scale).astype(jnp.bfloat16)
            value_grad = jnp.einsum('hqk,qhd->kd', weights, grad_block).astype(jnp.bfloat16)
            rot_grad = jnp.einsum('hqk,qhd->kd', dscore, query_block) * scale
            key_grad = unrotate(rot_grad, cosine, sine).astype(jnp.bfloat16)
            attended_heads.append(attended.reshape(GROUP, per_group * HEAD))
            query_heads.append(query_grad.reshape(GROUP, per_group * HEAD))
            value_heads.append(value_grad)
            key_heads.append(key_grad)
        attended_groups.append(jnp.concatenate(attended_heads, axis=1))
        query_groups.append(jnp.concatenate(query_heads, axis=1))
        value_groups.append(jnp.concatenate(value_heads, axis=1))
        key_groups.append(jnp.concatenate(key_heads, axis=1))
    attended_all = jnp.concatenate(attended_groups, axis=0)
    query_all = jnp.concatenate(query_groups, axis=0)
    value_all = jnp.concatenate(value_groups, axis=0)
    key_all = jnp.concatenate(key_groups, axis=0)
    feature_grad = jnp.dot(to_loader(key_all), key_weight, preferred_element_type=jnp.float32).astype(jnp.bfloat16)
    key_weight_grad = jnp.dot(key_all.T, features, preferred_element_type=jnp.float32)
    return attended_all, query_all, value_all, feature_grad, key_weight_grad
```

```python
import math

import jax
import jax.numpy as jnp
from jax import lax
from jax.sharding import PartitionSpec as P

HEAD = 128


theta_base = 500000.0
masked_score = -1e30


def rotary_tables(offsets):
    half_dim = HEAD // 2
    exponent = jnp.arange(half_dim, dtype=jnp.float32) * (2.0 / HEAD)
    frequency = jnp.exp(-exponent * math.log(theta_base))
    angle = offsets.astype(jnp.float32)[:, None] * frequency[None, :]
    return (jnp.cos(angle), jnp.sin(angle))


def rotate(inputs, cosine, sine):
    half_dim = HEAD // 2
    first_half = inputs[..., :half_dim]
    second_half = inputs[..., half_dim:]
    return jnp.concatenate(
        [first_half * cosine - second_half * sine, second_half * cosine + first_half * sine],
        axis=-1,
    )


def unrotate(grads, cosine, sine):
    half_dim = HEAD // 2
    first_half = grads[..., :half_dim]
    second_half = grads[..., half_dim:]
    return jnp.concatenate(
        [first_half * cosine + second_half * sine, second_half * cosine - first_half * sine],
        axis=-1,
    )


def outgoing(array, chosen_slab, is_live, slab_count):
    blocks = array.reshape(slab_count, -1, array.shape[-1])
    picked = jnp.take(blocks, chosen_slab, axis=0)
    return jnp.where(is_live[:, None, None] > 0, picked, jnp.zeros_like(picked))


def arrange(received, chosen_slab):
    return jnp.take(received, chosen_slab, axis=0).reshape(-1, received.shape[-1])


def project_keys(features, key_weight):
    partial_keys = jnp.einsum("td,kd->tk", features, key_weight, preferred_element_type=jnp.float32)
    own_keys = lax.psum_scatter(partial_keys, "tensor", scatter_dimension=1, tiled=True)
    return lax.optimization_barrier(own_keys.astype(jnp.bfloat16))


def gather_heads(key_grad):
    return lax.all_gather(key_grad, "tensor", axis=1, tiled=True)


def weight_grads(all_grads, features):
    terms = jnp.einsum("tk,td->kd", all_grads, features, preferred_element_type=jnp.float32)
    moved = lax.all_to_all(
        terms.astype(jnp.bfloat16), ("dp", "ctx"), split_axis=0, concat_axis=0, tiled=True
    )
    parts = moved.reshape(lax.axis_size(("dp", "ctx")), -1, moved.shape[-1])
    return jnp.sum(parts.astype(jnp.float32), axis=0)


def shards(tokens, queries, values, out_grad, key_weight, plan, lengths):
    loaders = lax.axis_size(("dp", "ctx"))
    myself = lax.axis_index(("dp", "ctx"))
    group_index = lax.axis_index("dp")
    place_index = lax.axis_index("ctx")
    slab_count = plan.shape[1]
    local_rows = tokens.shape[0]
    heads_here = queries.shape[1] // HEAD
    loader_ids = jnp.arange(loaders, dtype=jnp.int32)
    slab_ids = jnp.arange(slab_count, dtype=jnp.int32)
    my_dests = lax.dynamic_index_in_dim(plan, myself, 0, keepdims=False)
    sends_to = (my_dests[None, :] == loader_ids[:, None]).astype(jnp.int32)
    send_live = jnp.sum(sends_to, axis=1)
    send_slab = jnp.sum(sends_to * slab_ids[None, :], axis=1)
    recv_live = jnp.sum((plan == myself).astype(jnp.int32), axis=1)
    recv_rank = jnp.cumsum(recv_live) - 1
    slot_match = ((recv_rank[:, None] == slab_ids[None, :]) & (recv_live[:, None] > 0)).astype(
        jnp.int32
    )
    from_loader = jnp.sum(slot_match * loader_ids[:, None], axis=0)
    back_slab = jnp.clip(recv_rank, 0, slab_count - 1)

    def send_out(array):
        return outgoing(array, send_slab, send_live, slab_count)

    raw_key = project_keys(tokens, key_weight)
    grouped = jnp.concatenate([queries, out_grad, values, raw_key], axis=1)
    moved = lax.all_to_all(send_out(grouped), ("dp", "ctx"), split_axis=0, concat_axis=0, tiled=True)
    arranged = arrange(moved, from_loader)
    width = queries.shape[1]
    query_ctx = arranged[:, :width]
    grad_ctx = arranged[:, width : 2 * width]
    value_ctx = arranged[:, 2 * width : 2 * width + HEAD]
    key_proj = arranged[:, 2 * width + HEAD :]
    group_lengths = lax.dynamic_index_in_dim(lengths, group_index, 0, keepdims=False)
    group_ends = jnp.cumsum(group_lengths)
    position = place_index * local_rows + jnp.arange(local_rows, dtype=jnp.int32)
    seq_start = jnp.sum(
        group_lengths[None, :] * (group_ends[None, :] <= position[:, None]).astype(jnp.int32),
        axis=1,
    )
    cosine, sine = rotary_tables(position - seq_start)
    keys = rotate(key_proj.astype(jnp.float32), cosine, sine).astype(jnp.bfloat16)
    both = lax.all_gather(jnp.concatenate([keys, value_ctx], axis=1), "ctx", axis=0, tiled=True)
    all_keys, all_values = both[:, :HEAD], both[:, HEAD:]
    query_three = query_ctx.reshape(local_rows, heads_here, HEAD)
    grad_three = grad_ctx.reshape(local_rows, heads_here, HEAD)
    key_total = all_keys.shape[0]
    key_block = min(512, key_total)
    block_count = key_total // key_block
    block_offsets = jnp.arange(key_block, dtype=jnp.int32)
    scale = HEAD ** (-0.5)
    block_list = jnp.arange(block_count, dtype=jnp.int32)

    def block_scores(first_key):
        key_tile = lax.dynamic_slice_in_dim(all_keys, first_key, key_block, 0)
        scores = (
            jnp.einsum("qhd,kd->hqk", query_three, key_tile, preferred_element_type=jnp.float32)
            * scale
        )
        key_position = first_key + block_offsets
        visible = (key_position[None, :] <= position[:, None]) & (
            key_position[None, :] >= seq_start[:, None]
        )
        return (key_tile, scores, visible[None])

    def stat_step(carry, block_index):
        highest, summed = carry
        first_key = block_index * key_block
        key_tile, scores, visible = block_scores(first_key)
        new_high = jnp.maximum(highest, jnp.max(jnp.where(visible, scores, masked_score), axis=2))
        grown = jnp.sum(jnp.where(visible, jnp.exp(scores - new_high[..., None]), 0.0), axis=2)
        return ((new_high, summed * jnp.exp(highest - new_high) + grown), None)

    start_high = jnp.full((heads_here, local_rows), masked_score, jnp.float32)
    start_sum = jnp.zeros((heads_here, local_rows), jnp.float32)
    (highest, summed), _ = lax.scan(stat_step, (start_high, start_sum), block_list)
    log_total = highest + jnp.log(summed)

    def output_step(accum, block_index):
        first_key = block_index * key_block
        key_tile, scores, visible = block_scores(first_key)
        weights = jnp.where(visible, jnp.exp(scores - log_total[..., None]), 0.0).astype(
            jnp.bfloat16
        )
        value_tile = lax.dynamic_slice_in_dim(all_values, first_key, key_block, 0)
        return (
            accum
            + jnp.einsum("hqk,kd->qhd", weights, value_tile, preferred_element_type=jnp.float32),
            None,
        )

    out_accum, _ = lax.scan(
        output_step, jnp.zeros((local_rows, heads_here, HEAD), jnp.float32), block_list
    )
    attended = out_accum.astype(jnp.bfloat16)
    delta = jnp.sum(grad_three.astype(jnp.float32) * attended.astype(jnp.float32), axis=2).T

    def back_step(query_accum, block_index):
        first_key = block_index * key_block
        key_tile, scores, visible = block_scores(first_key)
        value_tile = lax.dynamic_slice_in_dim(all_values, first_key, key_block, 0)
        prob = jnp.where(visible, jnp.exp(scores - log_total[..., None]), 0.0)
        dprob = jnp.einsum(
            "qhd,kd->hqk", grad_three, value_tile, preferred_element_type=jnp.float32
        )
        dscore = (prob * (dprob - delta[..., None])).astype(jnp.bfloat16)
        new_accum = query_accum + jnp.einsum(
            "hqk,kd->qhd", dscore, key_tile, preferred_element_type=jnp.float32
        )
        key_term = (
            jnp.einsum("hqk,qhd->kd", dscore, query_three, preferred_element_type=jnp.float32)
            * scale
        )
        value_term = jnp.einsum(
            "hqk,qhd->kd", prob.astype(jnp.bfloat16), grad_three, preferred_element_type=jnp.float32
        )
        return (new_accum, jnp.concatenate([key_term, value_term], axis=1))

    query_accum, stacked = lax.scan(
        back_step, jnp.zeros((local_rows, heads_here, HEAD), jnp.float32), block_list
    )
    query_grad = (query_accum * scale).astype(jnp.bfloat16).reshape(local_rows, heads_here * HEAD)
    group_terms = stacked.reshape(key_total, 2 * HEAD)
    owned = lax.psum_scatter(
        group_terms.astype(jnp.bfloat16), "ctx", scatter_dimension=0, tiled=True
    ).astype(jnp.float32)
    key_grad = unrotate(owned[:, :HEAD], cosine, sine).astype(jnp.bfloat16)
    value_grad = owned[:, HEAD:].astype(jnp.bfloat16)
    returned = lax.all_to_all(
        outgoing(key_grad, back_slab, recv_live, slab_count),
        ("dp", "ctx"),
        split_axis=0,
        concat_axis=0,
        tiled=True,
    )
    all_grads = gather_heads(arrange(returned, my_dests))
    feature_grad = jnp.dot(all_grads, key_weight, preferred_element_type=jnp.float32).astype(
        jnp.bfloat16
    )
    key_weight_grad = weight_grads(all_grads, tokens)
    attended_flat = attended.reshape(local_rows, heads_here * HEAD)
    return (attended_flat, query_grad, value_grad, feature_grad, key_weight_grad)


def solution(mesh):
    placed = (
        P(("dp", "ctx"), "tensor"),
        P(("dp", "ctx"), "tensor"),
        P(("dp", "ctx"), "tensor"),
        P(("dp", "ctx"), "tensor"),
        P(None, "tensor"),
        P(),
        P(),
    )
    return jax.shard_map(
        shards,
        mesh=mesh,
        in_specs=placed,
        out_specs=(
            P(("dp", "ctx"), "tensor"),
            P(("dp", "ctx"), "tensor"),
            P(("dp", "ctx"), "tensor"),
            P(("dp", "ctx"), "tensor"),
            P(("dp", "ctx"), "tensor"),
        ),
        check_vma=False,
    )
```

```python
import math

import jax
import jax.numpy as jnp
import numpy as np
from jax import lax
from jax.experimental import pallas as pl
from jax.experimental.pallas import tpu as pltpu
from jax.sharding import PartitionSpec as P

F32, BF16 = jnp.float32, jnp.bfloat16
HEAD = 128
THETA = 500000.0
MESH = pl.DeviceIdType.MESH
Q, KV, DO, PART, GATHER, TERMS, ZBACK, CBACK, KEYS, TOK, ZSUM, XSUM = range(12)
PHASES = 12
L_TOK, L_W, L_Q, L_V, L_DO, L_ATT, L_QG, L_VG, L_FG, L_KWG = range(10)


def iota(shape, axis):
    return lax.broadcasted_iota(jnp.int32, shape, axis)


def one_hot(mask):
    return jnp.where(mask, 1.0, 0.0).astype(BF16)


def mm(a, b):
    return lax.dot_general(a, b, (((1,), (0,)), ((), ())), preferred_element_type=F32)


def mm_nt(a, b):
    return lax.dot_general(a, b, (((1,), (1,)), ((), ())), preferred_element_type=F32)


def mm_tn(a, b):
    return lax.dot_general(a, b, (((0,), (0,)), ((), ())), preferred_element_type=F32)


def rows(start, size, step):
    return pl.ds(pl.multiple_of(start, step), size)


def kernel(
    plan, lengths, freq, tokens_h, q_h, v_h, do_h, w_h,
    att_h, qg_h, vg_h, fg_h, kwg_h,
    tok, qv, vv, dov, wv, smat, rmat,
    send_q, recv_q, send_do, recv_do, send_kv, recv_kv, part_s, part_r,
    kv_all, q_ctx, do_ctx, att, qg, terms, terms_s, terms_r,
    zs, zr, cs, cr, kgs, kgr, toks, sum_s, sum_r, xs, xr, vg, fg, kwg,
    local_sem, send_sem, recv_sem,
):
    d, c, t = lax.axis_index("dp"), lax.axis_index("ctx"), lax.axis_index("tensor")
    me = d * 8 + c
    x, y = lax.div(c, 4), lax.rem(c, 4)

    barrier = pltpu.get_barrier_semaphore()

    def greet_group(k, carry):
        peer = lax.rem(me + k, 64)
        pl.semaphore_signal(
            barrier, inc=1, device_id=(lax.div(peer, 8), lax.rem(peer, 8), t), device_id_type=MESH
        )
        return carry

    def greet_heads(k, carry):
        pl.semaphore_signal(
            barrier,
            inc=1,
            device_id=(d, lax.rem(k, 8), lax.rem(t + 1 + lax.div(k, 8), 4)),
            device_id_type=MESH,
        )
        return carry

    lax.fori_loop(1, 64, greet_group, 0)
    lax.fori_loop(0, 24, greet_heads, 0)

    def load(src, dst, k):
        return pltpu.make_async_copy(src, dst, local_sem.at[k])

    loads = {
        L_Q: load(q_h, qv, L_Q),
        L_TOK: load(tokens_h, tok, L_TOK),
        L_W: load(w_h, wv, L_W),
        L_V: load(v_h, vv, L_V),
        L_DO: load(do_h, dov, L_DO),
    }
    for item in loads.values():
        item.start()

    def remote(src, dst, phase, target):
        return pltpu.make_async_remote_copy(
            src_ref=src,
            dst_ref=dst,
            send_sem=send_sem.at[phase],
            recv_sem=recv_sem.at[phase],
            device_id=target,
            device_id_type=MESH,
        )

    def bulk(view, phase):
        return remote(view, view, phase, (d, lax.rem(c + 1, 8), t))

    row = plan[pl.ds(me, 1), :].astype(F32)
    spread = one_hot(lax.div(lax.rem(iota((32, 512), 1), 128), 4) == iota((32, 512), 0))
    dest = mm(jnp.broadcast_to(row, (128, 32)).astype(BF16), spread)
    r_row, r_col = iota((128, 512), 0), iota((128, 512), 1)
    fits = (lax.rem(r_row, 4) == lax.rem(r_col, 4)) & (
        lax.div(lax.rem(r_row, 16), 4) == lax.div(r_col, 128)
    )
    dest = jnp.where(fits, dest, -1.0)
    slot_row = lax.div(r_row, 16)

    loads[L_Q].wait()
    pl.semaphore_wait(barrier, 87)

    def send_slots(source, target, width, phase, off):
        g = lax.rem(d + off, 8)

        def one(k, carry):
            cc = lax.rem(c + k, 8)
            j = g * 8 + cc

            @pl.when((off > 0) | (k > 0))
            def _():
                remote(
                    source.at[rows(j * 16, 16, 16), :],
                    target.at[rows(me * 16, 16, 16), :],
                    phase,
                    (g, cc, t),
                ).start()

            return carry

        lax.fori_loop(0, 8, one, 0)

    def own_slot(source, target):
        target[rows(me * 16, 16, 16), :] = source[rows(me * 16, 16, 16), :]

    def send_queries(off, carry):
        g = lax.rem(d + off, 8)
        chosen = one_hot(dest == (slot_row + g * 8).astype(F32))
        smat[rows(g * 128, 128, 128), :] = chosen
        total = mm(chosen[:, 0:128], qv[:, 0:256])
        for ch in range(1, 4):
            total += mm(chosen[:, ch * 128 : ch * 128 + 128], qv[:, ch * 256 : ch * 256 + 256])
        send_q[rows(g * 128, 128, 128), :] = total.astype(BF16)
        send_slots(send_q, recv_q, 256, Q, off)
        return carry

    lax.fori_loop(0, 8, send_queries, 0)
    own_slot(send_q, recv_q)

    loads[L_TOK].wait()
    loads[L_W].wait()
    for h in range(4):
        part_s[h] = mm_nt(tok[...], wv[h * 128 : h * 128 + 128, :])

    def send_part(k, carry):
        tt = lax.rem(t + k, 4)
        remote(part_s.at[tt], part_r.at[t], PART, (d, c, tt)).start()
        return carry

    lax.fori_loop(1, 4, send_part, 0)
    part_r[pl.ds(t, 1)] = part_s[pl.ds(t, 1)]

    lens = lengths[...]
    high = lax.div(lens, 32)
    low = lens - high * 32
    upper = one_hot(iota((16, 16), 0) <= iota((16, 16), 1))
    ends = mm(high.astype(F32).astype(BF16), upper) * 32.0 + mm(low.astype(F32).astype(BF16), upper)
    mine = iota((8, 16), 0) == d
    end_row = jnp.sum(jnp.where(mine, ends, 0.0), axis=0, keepdims=True)
    len_row = jnp.sum(jnp.where(mine, lens.astype(F32), 0.0), axis=0, keepdims=True)
    position = (c * 128 + iota((128, 16), 0)).astype(F32)
    seq_start = jnp.sum(jnp.where(end_row <= position, len_row, 0.0), axis=1, keepdims=True)
    angle = (position[:, 0:1] - seq_start) * freq[...]
    cosine = jnp.cos(angle)
    sine = jnp.sin(angle)
    signed = jnp.where(iota((128, 128), 1) < 64, -sine, sine)

    loads[L_V].wait()
    loads[L_DO].wait()

    def send_cotangents(off, carry):
        g = lax.rem(d + off, 8)
        chosen = smat[rows(g * 128, 128, 128), :]
        total = mm(chosen[:, 0:128], dov[:, 0:256])
        for ch in range(1, 4):
            total += mm(chosen[:, ch * 128 : ch * 128 + 128], dov[:, ch * 256 : ch * 256 + 256])
        send_do[rows(g * 128, 128, 128), :] = total.astype(BF16)
        return carry

    lax.fori_loop(0, 8, send_cotangents, 0)

    bulk(part_r.at[pl.ds(0, 3)], PART).wait_recv()
    key_proj = (part_r[0] + part_r[1] + part_r[2] + part_r[3]).astype(BF16)

    def send_keys(off, carry):
        g = lax.rem(d + off, 8)
        chosen = smat[rows(g * 128, 128, 128), 0:256]
        total = mm(chosen[:, 0:128], key_proj) + mm(chosen[:, 128:256], vv[...])
        send_kv[rows(g * 128, 128, 128), :] = total.astype(BF16)
        send_slots(send_kv, recv_kv, 128, KV, off)
        return carry

    lax.fori_loop(0, 8, send_keys, 0)
    own_slot(send_kv, recv_kv)

    def start_cotangents(off, carry):
        send_slots(send_do, recv_do, 256, DO, off)
        return carry

    lax.fori_loop(0, 8, start_cotangents, 0)
    own_slot(send_do, recv_do)

    def send_tokens(k, carry):
        cc = lax.rem(c + k, 8)
        half = lax.div(cc, 4) * 1024
        remote(
            tok.at[:, rows(half, 1024, 128)],
            toks.at[rows(c * 128, 128, 128), :],
            TOK,
            (d, cc, t),
        ).start()
        return carry

    lax.fori_loop(1, 8, send_tokens, 0)
    toks[rows(c * 128, 128, 128), :] = tok[:, rows(x * 1024, 1024, 128)]

    live = jnp.sum(jnp.where(plan[...] == me, 1.0, 0.0), axis=1, keepdims=True)
    live = jnp.broadcast_to(live, (64, 128)).astype(BF16)
    slot = lax.div(iota((64, 1024), 1), 16)
    before = one_hot(iota((64, 1024), 0) < slot)
    same = one_hot(iota((64, 1024), 0) == slot)
    col = iota((128, 1024), 1)
    spot = mm_tn(live, before) * 4.0 + (
        lax.rem(col, 4) + 128 * lax.div(lax.rem(col, 16), 4)
    ).astype(F32)
    spot = jnp.where(mm_tn(live, same) > 0.5, spot, -1.0)
    for ch in range(4):
        rmat[ch * 128 : ch * 128 + 128, :] = one_hot(
            spot == (iota((128, 1024), 0) + ch * 128).astype(F32)
        )
    slot4 = lax.div(iota((64, 256), 1), 4)
    spot4 = mm_tn(live, one_hot(iota((64, 256), 0) < slot4)) * 4.0 + lax.rem(
        iota((128, 256), 1), 4
    ).astype(F32)
    spot4 = jnp.where(mm_tn(live, one_hot(iota((64, 256), 0) == slot4)) > 0.5, spot4, -1.0)
    back = one_hot(spot4 == iota((128, 256), 0).astype(F32))

    bulk(recv_kv.at[pl.ds(0, 1008)], KV).wait_recv()
    pair = mm(rmat[0:256, :], recv_kv[...])
    raw = pair[0:128]
    keys = raw * cosine + pltpu.roll(raw, 64, 1) * signed
    kv_all[rows(c * 128, 128, 128), 0:128] = keys.astype(BF16)
    kv_all[rows(c * 128, 128, 128), 128:256] = pair[128:256].astype(BF16)

    def send_gather(k, carry):
        cc = lax.rem(c + k, 8)
        block = kv_all.at[rows(c * 128, 128, 128), :]
        remote(block, block, GATHER, (d, cc, t)).start()
        return carry

    lax.fori_loop(1, 8, send_gather, 0)

    bulk(recv_q.at[pl.ds(0, 1008)], Q).wait_recv()
    for ch in range(4):
        q_ctx[:, ch * 256 : ch * 256 + 256] = mm(
            rmat[ch * 128 : ch * 128 + 128, :], recv_q[...]
        ).astype(BF16)
    bulk(recv_do.at[pl.ds(0, 1008)], DO).wait_recv()
    for ch in range(4):
        do_ctx[:, ch * 256 : ch * 256 + 256] = mm(
            rmat[ch * 128 : ch * 128 + 128, :], recv_do[...]
        ).astype(BF16)
    bulk(kv_all.at[pl.ds(0, 896)], GATHER).wait_recv()

    scale = HEAD**-0.5
    key_at = iota((128, 1024), 1).astype(F32)
    visible = (key_at <= (c * 128 + iota((128, 1024), 0)).astype(F32)) & (key_at >= seq_start)
    terms[...] = jnp.zeros_like(terms)

    def attend(h, carry):
        here = rows(h * 128, 128, 128)
        query, grad = q_ctx[:, here], do_ctx[:, here]
        key, value = kv_all[:, 0:128], kv_all[:, 128:256]
        scores = jnp.where(visible, mm_nt(query, key) * scale, -1e30)
        weight = jnp.where(visible, jnp.exp(scores - jnp.max(scores, axis=1, keepdims=True)), 0.0)
        prob = weight * (1.0 / jnp.sum(weight, axis=1, keepdims=True))
        rounded = prob.astype(BF16)
        out = mm(rounded, value).astype(BF16)
        att[:, here] = out
        delta = jnp.sum(grad.astype(F32) * out.astype(F32), axis=1, keepdims=True)
        dscore = (prob * (mm_nt(grad, value) - delta)).astype(BF16)
        qg[:, here] = (mm(dscore, key) * scale).astype(BF16)
        terms[:, 0:128] += mm_tn(dscore, query)
        terms[:, 128:256] += mm_tn(rounded, grad)
        return carry

    lax.fori_loop(0, 8, attend, 0)
    stores = {L_ATT: load(att, att_h, L_ATT), L_QG: load(qg, qg_h, L_QG)}
    stores[L_ATT].start()
    stores[L_QG].start()

    terms_s[...] = terms[...].astype(BF16)

    def send_terms(k, carry):
        cc = lax.rem(c + k, 8)
        remote(
            terms_s.at[rows(cc * 128, 128, 128), :],
            terms_r.at[rows(c * 128, 128, 128), :],
            TERMS,
            (d, cc, t),
        ).start()
        return carry

    lax.fori_loop(1, 8, send_terms, 0)
    terms_r[rows(c * 128, 128, 128), :] = terms_s[rows(c * 128, 128, 128), :]
    out_row, in_row = iota((256, 256), 0), iota((256, 256), 1)
    regroup = one_hot(
        (lax.div(out_row, 32) == lax.div(lax.rem(in_row, 32), 4))
        & (lax.div(lax.rem(out_row, 32), 4) == lax.div(in_row, 32))
        & (lax.rem(out_row, 4) == lax.rem(in_row, 4))
    )
    line = iota((256, 128), 0)
    source = lax.div(lax.rem(line, 32), 4) * 8 + lax.div(line, 32)
    spread4 = one_hot(lax.div(iota((32, 128), 1), 4) == iota((32, 128), 0))
    dest4 = mm(jnp.broadcast_to(row, (256, 32)).astype(BF16), spread4)
    collect = one_hot(
        (dest4 == source.astype(F32)) & (lax.rem(line, 4) == lax.rem(iota((256, 128), 1), 4))
    )
    new_col, old = iota((512, 512), 1), iota((512, 512), 0)
    reorder = one_hot(
        old
        == lax.rem(lax.div(new_col, 16), 8) * 64
        + lax.rem(lax.div(new_col, 8), 2) * 32
        + lax.div(new_col, 128) * 8
        + lax.rem(new_col, 8)
    )
    bulk(terms_r.at[pl.ds(0, 896)], TERMS).wait_recv()
    owned = terms_r[0:128, :].astype(F32)
    for k in range(1, 8):
        owned += terms_r[k * 128 : k * 128 + 128, :].astype(F32)
    rot_grad = owned[:, 0:128] * scale
    vg[...] = owned[:, 128:256].astype(BF16)
    stores[L_VG] = load(vg, vg_h, L_VG)
    stores[L_VG].start()
    key_grad = (rot_grad * cosine - pltpu.roll(rot_grad, 64, 1) * signed).astype(BF16)

    zs[...] = mm_tn(back, key_grad).astype(BF16)

    def send_z(k, carry):
        g = lax.rem(d + k, 8)
        remote(
            zs.at[rows(g * 32, 32, 32), :], zr.at[rows(d * 32, 32, 32), :], ZBACK, (g, c, t)
        ).start()
        return carry

    lax.fori_loop(1, 8, send_z, 0)
    zr[rows(d * 32, 32, 32), :] = zs[rows(d * 32, 32, 32), :]
    bulk(zr.at[pl.ds(0, 224)], ZBACK).wait_recv()
    cs[...] = mm(regroup, zr[...]).astype(BF16)
    spot_here = t * 256 + c * 32

    def send_c(k, carry):
        cc = lax.rem(c + lax.rem(k, 8), 8)
        tt = lax.rem(t + lax.div(k, 8), 4)
        remote(
            cs.at[rows(cc * 32, 32, 32), :], cr.at[rows(spot_here, 32, 32), :], CBACK, (d, cc, tt)
        ).start()
        return carry

    lax.fori_loop(1, 32, send_c, 0)
    cr[rows(spot_here, 32, 32), :] = cs[rows(c * 32, 32, 32), :]
    bulk(cr.at[pl.ds(0, 992)], CBACK).wait_recv()
    all_grads = jnp.concatenate(
        [mm_tn(collect, cr[h * 256 : h * 256 + 256, :]).astype(BF16) for h in range(4)], axis=1
    )

    moved = mm(all_grads, reorder).astype(BF16)
    for k in range(4):
        kgs[k] = moved[:, k * 128 : k * 128 + 128]

    def send_grads(k, carry):
        cc = lax.rem(c + k, 8)
        remote(
            kgs.at[lax.rem(cc, 4)], kgr.at[rows(c * 128, 128, 128), :], KEYS, (d, cc, t)
        ).start()
        return carry

    lax.fori_loop(1, 8, send_grads, 0)
    kgr[rows(c * 128, 128, 128), :] = kgs[y]
    for k in range(4):
        fg[:, k * 512 : k * 512 + 512] = mm(
            all_grads, wv[:, k * 512 : k * 512 + 512]
        ).astype(BF16)
    stores[L_FG] = load(fg, fg_h, L_FG)
    stores[L_FG].start()
    bulk(toks.at[pl.ds(0, 896)], TOK).wait_recv()
    bulk(kgr.at[pl.ds(0, 896)], KEYS).wait_recv()
    sum_s[...] = mm_tn(kgr[...], toks[...]).astype(BF16)

    def send_sums(k, carry):
        g = lax.rem(d + k, 8)
        remote(
            sum_s.at[rows(g * 16, 16, 16), :], sum_r.at[rows(d * 16, 16, 16), :], ZSUM, (g, c, t)
        ).start()
        return carry

    lax.fori_loop(1, 8, send_sums, 0)
    sum_r[rows(d * 16, 16, 16), :] = sum_s[rows(d * 16, 16, 16), :]
    bulk(sum_r.at[pl.ds(0, 112)], ZSUM).wait_recv()
    added = sum_r[0:16, :].astype(F32)
    for k in range(1, 8):
        added += sum_r[k * 16 : k * 16 + 16, :].astype(F32)
    xs[0] = added[0:8]
    xs[1] = added[8:16]
    swap = remote(xs.at[1 - x], xr, XSUM, (d, lax.rem(c + 4, 8), t))
    swap.start()
    kwg[:, rows(x * 1024, 1024, 128)] = xs[x]
    swap.wait_recv()
    kwg[:, rows((1 - x) * 1024, 1024, 128)] = xr[...]
    stores[L_KWG] = load(kwg, kwg_h, L_KWG)
    stores[L_KWG].start()

    bulk(send_q.at[pl.ds(0, 1008)], Q).wait_send()
    bulk(send_kv.at[pl.ds(0, 1008)], KV).wait_send()
    bulk(send_do.at[pl.ds(0, 1008)], DO).wait_send()
    bulk(part_s.at[pl.ds(0, 3)], PART).wait_send()
    bulk(kv_all.at[pl.ds(0, 896)], GATHER).wait_send()
    bulk(terms_s.at[pl.ds(0, 896)], TERMS).wait_send()
    bulk(zs.at[pl.ds(0, 224)], ZBACK).wait_send()
    bulk(cr.at[pl.ds(0, 992)], CBACK).wait_send()
    bulk(kgr.at[pl.ds(0, 896)], KEYS).wait_send()
    bulk(toks.at[pl.ds(0, 896)], TOK).wait_send()
    bulk(sum_s.at[pl.ds(0, 112)], ZSUM).wait_send()
    swap.wait_send()
    for item in stores.values():
        item.wait()


def shards(tokens, queries, values, out_grad, key_weight, plan, lengths):
    half = np.arange(128) % 64
    freq = np.exp(-(half.astype(np.float32) * np.float32(2.0 / HEAD)) * np.float32(math.log(THETA)))
    freq = jnp.asarray(freq.astype(np.float32).reshape(1, 128))
    vmem = pl.BlockSpec(memory_space=pltpu.VMEM)
    hbm = pl.BlockSpec(memory_space=pl.ANY)
    scratch = [
        ((128, 2048), BF16), ((128, 1024), BF16), ((128, 128), BF16), ((128, 1024), BF16),
        ((512, 2048), BF16), ((1024, 512), BF16), ((512, 1024), BF16),
        ((1024, 256), BF16), ((1024, 256), BF16), ((1024, 256), BF16), ((1024, 256), BF16),
        ((1024, 128), BF16), ((1024, 128), BF16), ((4, 128, 128), F32), ((4, 128, 128), F32),
        ((1024, 256), BF16), ((128, 1024), BF16), ((128, 1024), BF16), ((128, 1024), BF16),
        ((128, 1024), BF16), ((1024, 256), F32), ((1024, 256), BF16), ((1024, 256), BF16),
        ((256, 128), BF16), ((256, 128), BF16), ((256, 128), BF16), ((1024, 128), BF16),
        ((4, 128, 128), BF16), ((1024, 128), BF16), ((1024, 1024), BF16), ((128, 1024), BF16),
        ((128, 1024), BF16), ((2, 8, 1024), F32), ((8, 1024), F32), ((128, 128), BF16),
        ((128, 2048), BF16), ((8, 2048), F32),
    ]
    return pl.pallas_call(
        kernel,
        out_shape=(
            jax.ShapeDtypeStruct((128, 1024), BF16),
            jax.ShapeDtypeStruct((128, 1024), BF16),
            jax.ShapeDtypeStruct((128, 128), BF16),
            jax.ShapeDtypeStruct((128, 2048), BF16),
            jax.ShapeDtypeStruct((8, 2048), F32),
        ),
        in_specs=[vmem] * 3 + [hbm] * 5,
        out_specs=(hbm,) * 5,
        scratch_shapes=[pltpu.VMEM(shape, dtype) for shape, dtype in scratch]
        + [
            pltpu.SemaphoreType.DMA((10,)),
            pltpu.SemaphoreType.DMA((PHASES,)),
            pltpu.SemaphoreType.DMA((PHASES,)),
        ],
        compiler_params=pltpu.CompilerParams(
            collective_id=0, has_side_effects=True, vmem_limit_bytes=48 * 1024 * 1024
        ),
    )(plan, lengths, freq, tokens, queries, values, out_grad, key_weight)


def solution(mesh):
    both = P(("dp", "ctx"), "tensor")
    return jax.shard_map(
        shards,
        mesh=mesh,
        in_specs=(both, both, both, both, P(None, "tensor"), P(), P()),
        out_specs=(both,) * 5,
        check_vma=False,
    )
```

```python
import math

import jax
import jax.numpy as jnp
import numpy as np
from jax import lax
from jax.experimental import pallas as pl
from jax.experimental.pallas import tpu as pltpu
from jax.sharding import PartitionSpec as P

F32, BF16 = jnp.float32, jnp.bfloat16
HEAD = 128
THETA = 500000.0
MESH = pl.DeviceIdType.MESH
Q, ZKV, CKV, DO, PART, GATHER, TERMS, ZBACK, CBACK, KEYS, TOK, ZSUM, YSUM = range(13)
PHASES = 13
L_TOK, L_W, L_Q, L_V, L_DO, L_ATT, L_QG, L_VG, L_FG, L_KWG = range(10)


def iota(shape, axis):
    return lax.broadcasted_iota(jnp.int32, shape, axis)


def one_hot(mask):
    return jnp.where(mask, 1.0, 0.0).astype(BF16)


def mm(a, b):
    return lax.dot_general(a, b, (((1,), (0,)), ((), ())), preferred_element_type=F32)


def mm_nt(a, b):
    return lax.dot_general(a, b, (((1,), (1,)), ((), ())), preferred_element_type=F32)


def mm_tn(a, b):
    return lax.dot_general(a, b, (((0,), (0,)), ((), ())), preferred_element_type=F32)


def rows(start, size, step):
    return pl.ds(pl.multiple_of(start, step), size)


def kernel(
    plan, lengths, freq, tokens_h, q_h, v_h, do_h, w_h,
    att_h, qg_h, vg_h, fg_h, kwg_h,
    tok, qv, vv, dov, wv, smat, rmat,
    send_q, recv_q, send_do, recv_do, zkv_s, zkv_r, ckv_s, ckv_r, part_s, part_r,
    kv_all, qs, dos, prob, weights, dscores, att, att_t, delta, qg, terms_s, terms_r,
    zs, zr, cs, cr, kgs, kgr, toks, sum_s, sum_r, ys, yr, vg, fg, kwg,
    local_sem, send_sem, recv_sem, term_sem,
):
    d, c, t = lax.axis_index("dp"), lax.axis_index("ctx"), lax.axis_index("tensor")
    me = d * 8 + c
    x, y = lax.div(c, 4), lax.rem(c, 4)

    barrier = pltpu.get_barrier_semaphore()

    def greet_group(k, carry):
        peer = lax.rem(me + k, 64)
        pl.semaphore_signal(
            barrier, inc=1, device_id=(lax.div(peer, 8), lax.rem(peer, 8), t), device_id_type=MESH
        )
        return carry

    def greet_heads(k, carry):
        pl.semaphore_signal(
            barrier,
            inc=1,
            device_id=(d, lax.rem(k, 8), lax.rem(t + 1 + lax.div(k, 8), 4)),
            device_id_type=MESH,
        )
        return carry

    lax.fori_loop(1, 64, greet_group, 0)
    lax.fori_loop(0, 24, greet_heads, 0)

    def local(src, dst, k):
        return pltpu.make_async_copy(src, dst, local_sem.at[k])

    loads = {
        L_Q: local(q_h, qv, L_Q),
        L_TOK: local(tokens_h, tok, L_TOK),
        L_W: local(w_h, wv, L_W),
        L_V: local(v_h, vv, L_V),
        L_DO: local(do_h, dov, L_DO),
    }
    for item in loads.values():
        item.start()
    stores = {}

    def remote(src, dst, phase, target):
        return pltpu.make_async_remote_copy(
            src_ref=src,
            dst_ref=dst,
            send_sem=send_sem.at[phase],
            recv_sem=recv_sem.at[phase],
            device_id=target,
            device_id_type=MESH,
        )

    sizes = {
        Q: recv_q.at[pl.ds(0, 1008)],
        ZKV: zkv_r.at[pl.ds(0, 224)],
        CKV: ckv_r.at[pl.ds(0, 224)],
        DO: recv_do.at[pl.ds(0, 1008)],
        PART: part_r.at[pl.ds(0, 3)],
        GATHER: kv_all.at[pl.ds(0, 896)],
        ZBACK: zr.at[pl.ds(0, 224)],
        CBACK: kgr.at[pl.ds(0, 496)],
        KEYS: kgr.at[pl.ds(0, 896)],
        TOK: toks.at[pl.ds(0, 896)],
        ZSUM: sum_r.at[pl.ds(0, 224)],
        YSUM: yr.at[pl.ds(0, 3)],
    }
    unsent, unread = set(), set()

    def started(phase):
        unsent.add(phase)
        unread.add(phase)

    def bulk(phase):
        return remote(sizes[phase], sizes[phase], phase, (d, lax.rem(c + 1, 8), t))

    def arrived(phase):
        unread.discard(phase)
        bulk(phase).wait_recv()

    def term_copy(owner, k):
        return pltpu.make_async_remote_copy(
            src_ref=terms_s.at[rows(owner * 128, 128, 128), :],
            dst_ref=terms_r.at[rows(c * 128, 128, 128), :],
            send_sem=term_sem.at[0, owner],
            recv_sem=term_sem.at[1, c if k is None else k],
            device_id=(d, owner, t),
            device_id_type=MESH,
        )

    def finish():
        for phase in sorted(unread):
            bulk(phase).wait_recv()
        for phase in sorted(unsent):
            bulk(phase).wait_send()
        for item in (*loads.values(), *stores.values()):
            item.wait()

    row = jnp.sum(jnp.where(iota((32, 64), 1) == me, plan[...].astype(F32), 0.0), axis=1, keepdims=True)
    row = jnp.broadcast_to(row, (32, 256)).astype(BF16)
    spread = one_hot(lax.div(lax.rem(iota((32, 512), 1), 128), 4) == iota((32, 512), 0))
    dest = mm_tn(row, spread)
    r_row, r_col = iota((128, 512), 0), iota((128, 512), 1)
    fits = (lax.rem(r_row, 4) == lax.rem(r_col, 4)) & (
        lax.div(lax.rem(r_row, 16), 4) == lax.div(r_col, 128)
    )
    slotted = jnp.where(fits, dest[0:128], -1.0) - lax.div(r_row, 16).astype(F32)
    for g in range(8):
        smat[g * 128 : g * 128 + 128, :] = one_hot(slotted == g * 8.0)

    def stage(source):
        total = mm(smat[:, 0:128], source[:, 0:256])
        for ch in range(1, 4):
            total += mm(smat[:, ch * 128 : ch * 128 + 128], source[:, ch * 256 : ch * 256 + 256])
        return total.astype(BF16)

    loads.pop(L_Q).wait()
    send_q[...] = stage(qv)
    pl.semaphore_wait(barrier, 87)

    def send_slots(source, target, phase):
        def one(k, carry):
            peer = lax.rem(me + k, 64)
            remote(
                source.at[rows(peer * 16, 16, 16), :],
                target.at[rows(me * 16, 16, 16), :],
                phase,
                (lax.div(peer, 8), lax.rem(peer, 8), t),
            ).start()
            return carry

        lax.fori_loop(1, 64, one, 0)
        started(phase)
        target[rows(me * 16, 16, 16), :] = source[rows(me * 16, 16, 16), :]

    send_slots(send_q, recv_q, Q)

    loads.pop(L_TOK).wait()
    loads.pop(L_W).wait()
    for h in range(4):
        part_s[h] = mm_nt(tok[...], wv[h * 128 : h * 128 + 128, :])

    def send_part(k, carry):
        tt = lax.rem(t + k, 4)
        remote(part_s.at[tt], part_r.at[t], PART, (d, c, tt)).start()
        return carry

    lax.fori_loop(1, 4, send_part, 0)
    started(PART)
    part_r[pl.ds(t, 1)] = part_s[pl.ds(t, 1)]

    line, column = iota((256, 128), 0), iota((256, 128), 1)
    four = lax.rem(line, 4) == lax.rem(column, 4)
    to_slots = one_hot(four & (dest[:, 0:128] == lax.div(line, 4).astype(F32)))
    out_row, in_row = iota((256, 256), 0), iota((256, 256), 1)
    regroup = one_hot(
        (lax.div(out_row, 32) == lax.div(lax.rem(in_row, 32), 4))
        & (lax.div(lax.rem(out_row, 32), 4) == lax.div(in_row, 32))
        & (lax.rem(out_row, 4) == lax.rem(in_row, 4))
    )
    hits = one_hot(plan[...] == me)
    live_row = mm(jnp.ones((128, 32), BF16), hits).astype(BF16)
    live_col = mm_tn(hits, jnp.ones((32, 128), BF16)).astype(BF16)
    lane = iota((64, 256), 1)
    sender = lax.div(lax.rem(lane, 32), 4) * 8 + lax.div(lane, 32)
    order = iota((64, 256), 0)
    spot = mm(live_row, one_hot(order < sender)) * 4.0
    spot += lax.rem(iota((128, 256), 1), 4).astype(F32)
    spot = jnp.where(mm(live_row, one_hot(order == sender)) > 0.5, spot, -1.0)
    to_rows = one_hot(spot == iota((128, 256), 0).astype(F32))

    loads.pop(L_V).wait()
    loads.pop(L_DO).wait()
    send_do[...] = stage(dov)

    lens = lengths[...]
    high = lax.div(lens, 32)
    low = lens - high * 32
    upper = one_hot(iota((16, 16), 0) <= iota((16, 16), 1))
    ends = mm(high.astype(F32).astype(BF16), upper) * 32.0 + mm(low.astype(F32).astype(BF16), upper)
    mine = iota((8, 16), 0) == d
    end_row = jnp.sum(jnp.where(mine, ends, 0.0), axis=0, keepdims=True)
    len_row = jnp.sum(jnp.where(mine, lens.astype(F32), 0.0), axis=0, keepdims=True)
    position = (c * 128 + iota((128, 16), 0)).astype(F32)
    seq_start = jnp.sum(jnp.where(end_row <= position, len_row, 0.0), axis=1, keepdims=True)
    angle = (position[:, 0:1] - seq_start) * freq[...]
    cosine = jnp.cos(angle)
    sine = jnp.sin(angle)
    signed = jnp.where(iota((128, 128), 1) < 64, -sine, sine)

    arrived(PART)
    key_proj = (part_r[0] + part_r[1] + part_r[2] + part_r[3]).astype(BF16)
    zkv_s[...] = mm(to_slots, jnp.concatenate([key_proj, vv[...]], axis=1)).astype(BF16)

    def send_blocks(source, target, phase, size):
        def one(k, carry):
            g = lax.rem(d + k, 8)
            remote(
                source.at[rows(g * size, size, size), :],
                target.at[rows(d * size, size, size), :],
                phase,
                (g, c, t),
            ).start()
            return carry

        lax.fori_loop(1, 8, one, 0)
        started(phase)
        target[rows(d * size, size, size), :] = source[rows(d * size, size, size), :]

    send_blocks(zkv_s, zkv_r, ZKV, 32)
    send_slots(send_do, recv_do, DO)

    slot = lax.div(iota((64, 1024), 1), 16)
    col = iota((128, 1024), 1)
    spot = mm(live_row, one_hot(iota((64, 1024), 0) < slot)) * 4.0 + (
        lax.rem(col, 4) + 128 * lax.div(lax.rem(col, 16), 4)
    ).astype(F32)
    spot = jnp.where(mm(live_row, one_hot(iota((64, 1024), 0) == slot)) > 0.5, spot, -1.0)
    for ch in range(4):
        rmat[ch * 128 : ch * 128 + 128, :] = one_hot(
            spot == (iota((128, 1024), 0) + ch * 128).astype(F32)
        )

    arrived(ZKV)
    ckv_s[...] = mm(regroup, zkv_r[...]).astype(BF16)

    def send_ckv(k, carry):
        cc = lax.rem(c + k, 8)
        remote(
            ckv_s.at[rows(cc * 32, 32, 32), :], ckv_r.at[rows(c * 32, 32, 32), :], CKV, (d, cc, t)
        ).start()
        return carry

    lax.fori_loop(1, 8, send_ckv, 0)
    started(CKV)
    ckv_r[rows(c * 32, 32, 32), :] = ckv_s[rows(c * 32, 32, 32), :]
    for k in range(8):

        @pl.when(k < c)
        def _():
            terms_r[k * 128 : k * 128 + 128, :] = jnp.zeros((128, 256), BF16)

    arrived(CKV)
    pair = mm(to_rows, ckv_r[...])
    raw = pair[:, 0:128]
    keys = raw * cosine + pltpu.roll(raw, 64, 1) * signed
    kv_all[rows(c * 128, 128, 128), 0:128] = keys.astype(BF16)
    kv_all[rows(c * 128, 128, 128), 128:256] = pair[:, 128:256].astype(BF16)

    def send_gather(k, carry):
        cc = lax.rem(c + k, 8)
        block = kv_all.at[rows(c * 128, 128, 128), :]
        remote(block, block, GATHER, (d, cc, t)).start()
        return carry

    lax.fori_loop(1, 8, send_gather, 0)
    started(GATHER)

    def send_tokens(k, carry):
        cc = lax.rem(c + k, 8)
        remote(
            tok.at[:, rows(lax.rem(cc, 4) * 512, 512, 128)],
            toks.at[rows(c * 128, 128, 128), :],
            TOK,
            (d, cc, t),
        ).start()
        return carry

    lax.fori_loop(1, 8, send_tokens, 0)
    started(TOK)
    toks[rows(c * 128, 128, 128), :] = tok[:, rows(y * 512, 512, 128)]

    arrived(Q)
    heads = mm(rmat[...], recv_q[...]).astype(BF16)
    for ch in range(4):
        for k in range(2):
            qs[(2 * ch + k) * 128 : (2 * ch + k) * 128 + 128, :] = heads[
                ch * 128 : ch * 128 + 128, k * 128 : k * 128 + 128
            ]
    scale = HEAD**-0.5
    key_at = iota((1024, 128), 0).astype(F32)
    query_at = (c * 128 + iota((16, 128), 1)).astype(F32)
    end_all = jnp.where(mine, ends, 0.0)
    len_all = jnp.where(mine, lens.astype(F32), 0.0)
    pick = jnp.ones((8, 128), F32)
    end_col = lax.dot_general(
        end_all, pick, (((0,), (0,)), ((), ())),
        precision=lax.Precision.HIGHEST, preferred_element_type=F32,
    )
    len_col = lax.dot_general(
        len_all, pick, (((0,), (0,)), ((), ())),
        precision=lax.Precision.HIGHEST, preferred_element_type=F32,
    )
    starts = jnp.sum(jnp.where(end_col <= query_at, len_col, 0.0), axis=0, keepdims=True)
    hidden = jnp.where((key_at <= query_at[0:1]) & (key_at >= starts), 0.0, -1e30)

    arrived(GATHER)

    def forward(h, carry):
        here = rows(h * 128, 128, 128)
        scores = mm_nt(kv_all[:, 0:128], qs[here, :]) * scale + hidden
        grown = jnp.exp(scores - jnp.max(scores, axis=0, keepdims=True))
        chance = grown * (1.0 / jnp.sum(grown, axis=0, keepdims=True))
        prob[:, here] = chance
        rounded = chance.astype(BF16)
        weights[:, here] = rounded
        out = mm_tn(kv_all[:, 128:256], rounded).astype(BF16)
        att_t[:, here] = out
        att[:, here] = out.T
        return carry

    lax.fori_loop(0, 8, forward, 0)
    stores[L_ATT] = local(att, att_h, L_ATT)
    stores[L_ATT].start()

    arrived(DO)
    heads = mm(rmat[...], recv_do[...]).astype(BF16)
    for ch in range(4):
        for k in range(2):
            h = 2 * ch + k
            block = heads[ch * 128 : ch * 128 + 128, k * 128 : k * 128 + 128]
            dos[h * 128 : h * 128 + 128, :] = block
            products = block.T.astype(F32) * att_t[:, h * 128 : h * 128 + 128].astype(F32)
            delta[:, h * 128 : h * 128 + 128] = jnp.sum(products, axis=0, keepdims=True)

    def backward(k, carry):
        chunk = lax.rem(lax.div(c, 2) + 1 + k, 4)
        here = rows(chunk * 256, 256, 256)
        grads = mm_nt(kv_all[here, 128:256], dos[...]) - delta[...]
        rounded = (prob[here, :] * grads).astype(BF16)
        dscores[here, :] = rounded
        terms_s[here, 0:128] = mm(rounded, qs[...]).astype(BF16)
        terms_s[here, 128:256] = mm(weights[here, :], dos[...]).astype(BF16)
        for part in range(2):
            owner = chunk * 2 + part

            @pl.when(owner < c)
            def _():
                term_copy(owner, None).start()

        return carry

    lax.fori_loop(0, 4, backward, 0)
    terms_r[rows(c * 128, 128, 128), :] = terms_s[rows(c * 128, 128, 128), :]

    def query_grads(h, carry):
        here = rows(h * 128, 128, 128)
        grad = mm_tn(kv_all[:, 0:128], dscores[:, here]) * scale
        qg[:, here] = grad.astype(BF16).T
        return carry

    lax.fori_loop(0, 8, query_grads, 0)
    stores[L_QG] = local(qg, qg_h, L_QG)
    stores[L_QG].start()

    before = mm(one_hot(iota((64, 64), 1) < iota((64, 64), 0)), live_col).astype(BF16)
    widen = one_hot(iota((256, 64), 1) == lax.div(iota((256, 64), 0), 4))
    spot = mm(widen, before) * 4.0 + lax.rem(line, 4).astype(F32)
    spot = jnp.where(mm(widen, live_col) > 0.5, spot, -1.0)
    back = one_hot(spot == column.astype(F32))
    spread4 = one_hot(iota((128, 32), 1) == lax.div(iota((128, 32), 0), 4))
    lane = iota((128, 256), 1)
    sender = lax.div(lax.rem(lane, 32), 4) * 8 + lax.div(lane, 32)
    collect = one_hot(
        (mm(spread4, row) == sender.astype(F32))
        & (lax.rem(lane, 4) == lax.rem(iota((128, 256), 0), 4))
    )
    new_col, old = iota((512, 512), 1), iota((512, 512), 0)
    reorder = one_hot(
        old
        == lax.div(lax.rem(new_col, 256), 32) * 64
        + lax.div(new_col, 256) * 32
        + lax.rem(new_col, 32)
    )
    for k in range(8):

        @pl.when(k > c)
        def _():
            term_copy(k, k).wait_recv()

    owned = terms_r[0:128, :].astype(F32)
    for k in range(1, 8):
        owned += terms_r[k * 128 : k * 128 + 128, :].astype(F32)
    rot_grad = owned[:, 0:128] * scale
    key_grad = (rot_grad * cosine - pltpu.roll(rot_grad, 64, 1) * signed).astype(BF16)
    zs[...] = mm(back, key_grad).astype(BF16)
    send_blocks(zs, zr, ZBACK, 32)
    vg[...] = owned[:, 128:256].astype(BF16)
    stores[L_VG] = local(vg, vg_h, L_VG)
    stores[L_VG].start()
    arrived(ZBACK)
    cs[...] = mm(regroup, zr[...]).astype(BF16)

    def send_c(k, carry):
        cc = lax.rem(c + k, 8)
        tt = lax.rem(t + lax.div(k, 8), 4)
        remote(
            cs.at[rows(cc * 32, 32, 32), :],
            cr.at[rows(c * 32, 32, 32), rows(t * 128, 128, 128)],
            CBACK,
            (d, cc, tt),
        ).start()
        return carry

    lax.fori_loop(1, 32, send_c, 0)
    started(CBACK)
    cr[rows(c * 32, 32, 32), rows(t * 128, 128, 128)] = cs[rows(c * 32, 32, 32), :]
    arrived(CBACK)
    all_grads = mm(collect, cr[...]).astype(BF16)

    moved = mm(all_grads, reorder).astype(BF16)
    for k in range(2):
        kgs[k] = moved[:, k * 256 : k * 256 + 256]

    def send_grads(k, carry):
        cc = lax.rem(c + k, 8)
        remote(
            kgs.at[lax.div(cc, 4)], kgr.at[rows(c * 128, 128, 128), :], KEYS, (d, cc, t)
        ).start()
        return carry

    lax.fori_loop(1, 8, send_grads, 0)
    started(KEYS)
    kgr[rows(c * 128, 128, 128), :] = kgs[x]
    for k in range(4):
        fg[:, k * 512 : k * 512 + 512] = mm(
            all_grads, wv[:, k * 512 : k * 512 + 512]
        ).astype(BF16)
    stores[L_FG] = local(fg, fg_h, L_FG)
    stores[L_FG].start()
    arrived(TOK)
    arrived(KEYS)
    sum_s[...] = mm_tn(kgr[...], toks[...]).astype(BF16)
    send_blocks(sum_s, sum_r, ZSUM, 32)
    arrived(ZSUM)
    added = sum_r[0:32, :].astype(F32)
    for k in range(1, 8):
        added += sum_r[k * 32 : k * 32 + 32, :].astype(F32)
    for k in range(4):
        ys[k] = added[k * 8 : k * 8 + 8]

    def send_y(k, carry):
        yy = lax.rem(y + k, 4)
        remote(ys.at[yy], yr.at[y], YSUM, (d, x * 4 + yy, t)).start()
        return carry

    lax.fori_loop(1, 4, send_y, 0)
    started(YSUM)
    yr[y] = ys[y]
    arrived(YSUM)
    for k in range(4):
        kwg[:, k * 512 : k * 512 + 512] = yr[k]
    stores[L_KWG] = local(kwg, kwg_h, L_KWG)
    stores[L_KWG].start()
    for k in range(8):

        @pl.when(k < c)
        def _():
            term_copy(k, None).wait_send()

    finish()


def copy_out(*refs):
    sem = refs[15]
    reads = [pltpu.make_async_copy(refs[k], refs[10 + k], sem.at[0, k]) for k in range(5)]
    writes = [pltpu.make_async_copy(refs[10 + k], refs[5 + k], sem.at[1, k]) for k in range(5)]
    for item in reads:
        item.start()
    for read, write in zip(reads, writes):
        read.wait()
        write.start()
    for item in writes:
        item.wait()


def shards(tokens, queries, values, out_grad, key_weight, plan, lengths):
    half = np.arange(128) % 64
    freq = np.exp(-(half.astype(np.float32) * np.float32(2.0 / HEAD)) * np.float32(math.log(THETA)))
    freq = jnp.asarray(freq.astype(np.float32).reshape(1, 128))
    vmem = pl.BlockSpec(memory_space=pltpu.VMEM)
    hbm = pl.BlockSpec(memory_space=pl.ANY)
    scratch = [
        ((128, 2048), BF16), ((128, 1024), BF16), ((128, 128), BF16), ((128, 1024), BF16),
        ((512, 2048), BF16), ((1024, 512), BF16), ((512, 1024), BF16),
        ((1024, 256), BF16), ((1024, 256), BF16), ((1024, 256), BF16), ((1024, 256), BF16),
        ((256, 256), BF16), ((256, 256), BF16), ((256, 256), BF16), ((256, 256), BF16),
        ((4, 128, 128), F32), ((4, 128, 128), F32),
        ((1024, 256), BF16), ((1024, 128), BF16), ((1024, 128), BF16), ((1024, 1024), F32),
        ((1024, 1024), BF16), ((1024, 1024), BF16), ((128, 1024), BF16), ((128, 1024), BF16),
        ((1, 1024), F32), ((128, 1024), BF16), ((1024, 256), BF16), ((1024, 256), BF16),
        ((256, 128), BF16), ((256, 128), BF16), ((256, 128), BF16), ((256, 512), BF16),
        ((2, 128, 256), BF16), ((1024, 256), BF16), ((1024, 512), BF16), ((256, 512), BF16),
        ((256, 512), BF16), ((4, 8, 512), F32), ((4, 8, 512), F32), ((128, 128), BF16),
        ((128, 2048), BF16), ((8, 2048), F32),
    ]
    shapes = (
        jax.ShapeDtypeStruct((128, 1024), BF16),
        jax.ShapeDtypeStruct((128, 1024), BF16),
        jax.ShapeDtypeStruct((128, 128), BF16),
        jax.ShapeDtypeStruct((128, 2048), BF16),
        jax.ShapeDtypeStruct((8, 2048), F32),
    )
    results = pl.pallas_call(
        kernel,
        out_shape=shapes,
        in_specs=[vmem] * 3 + [hbm] * 5,
        out_specs=(hbm,) * 5,
        scratch_shapes=[pltpu.VMEM(shape, dtype) for shape, dtype in scratch]
        + [
            pltpu.SemaphoreType.DMA((10,)),
            pltpu.SemaphoreType.DMA((PHASES,)),
            pltpu.SemaphoreType.DMA((PHASES,)),
            pltpu.SemaphoreType.DMA((2, 8)),
        ],
        compiler_params=pltpu.CompilerParams(
            collective_id=0, has_side_effects=True, vmem_limit_bytes=62 * 1024 * 1024
        ),
    )(plan.T, lengths, freq, tokens, queries, values, out_grad, key_weight)
    return pl.pallas_call(
        copy_out,
        out_shape=shapes,
        in_specs=[hbm] * 5,
        out_specs=(hbm,) * 5,
        scratch_shapes=[pltpu.VMEM(item.shape, item.dtype) for item in shapes]
        + [pltpu.SemaphoreType.DMA((2, 5))],
        compiler_params=pltpu.CompilerParams(vmem_limit_bytes=62 * 1024 * 1024),
    )(*results)


def solution(mesh):
    both = P(("dp", "ctx"), "tensor")
    return jax.shard_map(
        shards,
        mesh=mesh,
        in_specs=(both, both, both, both, P(None, "tensor"), P(), P()),
        out_specs=(both,) * 5,
        check_vma=False,
    )
```

```python
import math

import jax
import jax.numpy as jnp
import numpy as np
from jax import lax
from jax.experimental import pallas as pl
from jax.experimental.pallas import tpu as pltpu
from jax.sharding import PartitionSpec as P

F32, BF16 = jnp.float32, jnp.bfloat16
HEAD = 128
THETA = 500000.0
LOG2E = math.log2(math.e)
MESH = pl.DeviceIdType.MESH
Q, ZKV, CKV, DO, PART, GATHER, BACK, KEYS, HEADS, TOK, ZSUM = range(11)
PHASES = 11
L_TOK, L_W, L_Q, L_V, L_DO, L_ATT, L_QG, L_VG, L_FG, L_KWG = range(10)


def iota(shape, axis):
    return lax.broadcasted_iota(jnp.int32, shape, axis)


def one_hot(mask):
    return jnp.where(mask, 1.0, 0.0).astype(BF16)


def mm(a, b):
    return lax.dot_general(a, b, (((1,), (0,)), ((), ())), preferred_element_type=F32)


def mm_nt(a, b):
    return lax.dot_general(a, b, (((1,), (1,)), ((), ())), preferred_element_type=F32)


def mm_tn(a, b):
    return lax.dot_general(a, b, (((0,), (0,)), ((), ())), preferred_element_type=F32)


def rows(start, size, step):
    return pl.ds(pl.multiple_of(start, step), size)


def kernel(
    plan, lengths, freq, tokens_h, q_h, v_h, do_h, w_h,
    att_h, qg_h, vg_h, fg_h, kwg_h,
    tok, qv, vv, dov, wv, smat, rmat,
    send_q, recv_q, send_do, recv_do, zkv_s, zkv_r, ckv_s, ckv_r, part_s, part_r,
    kv_all, key_t, value_t, qs, dos, prob, weights, dscores, att, att_t, delta, qg,
    terms_s, terms_r, back, collect, back_s, back_r, kgs, kgr, toks, sum_s, sum_r,
    fg_s, fg_r, vg, fg, kwg,
    local_sem, send_sem, recv_sem, term_sem,
):
    d, c, t = lax.axis_index("dp"), lax.axis_index("ctx"), lax.axis_index("tensor")
    me = d * 8 + c
    x, y = lax.div(c, 4), lax.rem(c, 4)

    barrier = pltpu.get_barrier_semaphore()

    def greet_group(k, carry):
        peer = lax.rem(me + k, 64)
        pl.semaphore_signal(
            barrier, inc=1, device_id=(lax.div(peer, 8), lax.rem(peer, 8), t), device_id_type=MESH
        )
        return carry

    def greet_heads(k, carry):
        pl.semaphore_signal(
            barrier,
            inc=1,
            device_id=(d, lax.rem(k, 8), lax.rem(t + 1 + lax.div(k, 8), 4)),
            device_id_type=MESH,
        )
        return carry

    lax.fori_loop(1, 64, greet_group, 0)
    lax.fori_loop(0, 24, greet_heads, 0)

    def local(src, dst, k):
        return pltpu.make_async_copy(src, dst, local_sem.at[k])

    loads = {
        L_Q: local(q_h, qv, L_Q),
        L_TOK: local(tokens_h, tok, L_TOK),
        L_W: local(w_h, wv, L_W),
        L_V: local(v_h, vv, L_V),
        L_DO: local(do_h, dov, L_DO),
    }
    for item in loads.values():
        item.start()
    stores = {}

    def remote(src, dst, phase, target):
        return pltpu.make_async_remote_copy(
            src_ref=src,
            dst_ref=dst,
            send_sem=send_sem.at[phase],
            recv_sem=recv_sem.at[phase],
            device_id=target,
            device_id_type=MESH,
        )

    sizes = {
        Q: recv_q.at[pl.ds(0, 1008)],
        ZKV: zkv_r.at[pl.ds(0, 224)],
        CKV: ckv_r.at[pl.ds(0, 224)],
        DO: recv_do.at[pl.ds(0, 1008)],
        PART: part_r.at[pl.ds(0, 3)],
        GATHER: kv_all.at[pl.ds(0, 896)],
        BACK: back_r.at[pl.ds(0, 1008)],
        KEYS: kgr.at[pl.ds(0, 496)],
        HEADS: fg_r.at[pl.ds(0, 96)],
        TOK: toks.at[:, pl.ds(0, 448)],
        ZSUM: sum_r.at[pl.ds(0, 496)],
    }
    unsent, unread = set(), set()

    def started(phase):
        unsent.add(phase)
        unread.add(phase)

    def bulk(phase):
        return remote(sizes[phase], sizes[phase], phase, (d, lax.rem(c + 1, 8), t))

    def arrived(phase):
        unread.discard(phase)
        bulk(phase).wait_recv()

    def term_copy(owner, k):
        return pltpu.make_async_remote_copy(
            src_ref=terms_s.at[rows(owner * 128, 128, 128), :],
            dst_ref=terms_r.at[rows(c * 128, 128, 128), :],
            send_sem=term_sem.at[0, owner],
            recv_sem=term_sem.at[1, c if k is None else k],
            device_id=(d, owner, t),
            device_id_type=MESH,
        )

    def finish():
        for phase in sorted(unread):
            bulk(phase).wait_recv()
        for phase in sorted(unsent):
            bulk(phase).wait_send()
        for item in (*loads.values(), *stores.values()):
            item.wait()

    row = jnp.sum(jnp.where(iota((32, 64), 1) == me, plan[...].astype(F32), 0.0), axis=1, keepdims=True)
    row = jnp.broadcast_to(row, (32, 256)).astype(BF16)
    spread = one_hot(lax.div(lax.rem(iota((32, 512), 1), 128), 4) == iota((32, 512), 0))
    dest = mm_tn(row, spread)
    r_row, r_col = iota((128, 512), 0), iota((128, 512), 1)
    fits = (lax.rem(r_row, 4) == lax.rem(r_col, 4)) & (
        lax.div(lax.rem(r_row, 16), 4) == lax.div(r_col, 128)
    )
    slotted = jnp.where(fits, dest[0:128], -1.0) - lax.div(r_row, 16).astype(F32)
    for g in range(8):
        smat[g * 128 : g * 128 + 128, :] = one_hot(slotted == g * 8.0)

    def stage(source):
        total = mm(smat[:, 0:128], source[:, 0:256])
        for ch in range(1, 4):
            total += mm(smat[:, ch * 128 : ch * 128 + 128], source[:, ch * 256 : ch * 256 + 256])
        return total.astype(BF16)

    loads.pop(L_Q).wait()
    send_q[...] = stage(qv)
    loads.pop(L_TOK).wait()
    loads.pop(L_W).wait()
    for h in range(4):
        part_s[h] = mm_nt(tok[...], wv[h * 128 : h * 128 + 128, :])
    pl.semaphore_wait(barrier, 87)

    def send_part(k, carry):
        tt = lax.rem(t + k, 4)
        remote(part_s.at[tt], part_r.at[t], PART, (d, c, tt)).start()
        return carry

    lax.fori_loop(1, 4, send_part, 0)
    started(PART)
    part_r[pl.ds(t, 1)] = part_s[pl.ds(t, 1)]

    def far_first(k, places):
        m = lax.rem(k, 8)
        near = lax.div(m + 1, 2)
        ahead = jnp.where(lax.rem(m, 2) == 1, 4 - near, 4 + near)
        return lax.rem(d + ahead, 8), lax.rem(lax.div(k, 8) + m + 2, places)

    def send_slots(source, target, phase, low, high):
        def one(k, carry):
            g, away = far_first(k, 8)
            cc = lax.rem(c + away, 8)
            remote(
                source.at[rows((g * 8 + cc) * 16, 16, 16), :],
                target.at[rows(me * 16, 16, 16), :],
                phase,
                (g, cc, t),
            ).start()
            return carry

        lax.fori_loop(low, high, one, 0)

    def own_slot(source, target):
        target[rows(me * 16, 16, 16), :] = source[rows(me * 16, 16, 16), :]

    send_slots(send_q, recv_q, Q, 0, 32)

    def send_tokens(k, carry):
        cc = lax.rem(c + k, 8)
        for part in range(2):
            remote(
                tok.at[pl.ds(part * 64, 64), rows(lax.rem(cc, 4) * 512, 512, 128)],
                toks.at[part, rows(c * 64, 64, 64), :],
                TOK,
                (d, cc, t),
            ).start()
        return carry

    lax.fori_loop(1, 3, send_tokens, 0)
    for part in range(2):
        toks[part, rows(c * 64, 64, 64), :] = tok[
            part * 64 : part * 64 + 64, rows(y * 512, 512, 128)
        ]
    line, column = iota((256, 128), 0), iota((256, 128), 1)
    four = lax.rem(line, 4) == lax.rem(column, 4)
    to_slots = one_hot(four & (dest[:, 0:128] == lax.div(line, 4).astype(F32)))
    out_row, in_row = iota((256, 256), 0), iota((256, 256), 1)
    regroup = one_hot(
        (lax.div(out_row, 32) == lax.div(lax.rem(in_row, 32), 4))
        & (lax.div(lax.rem(out_row, 32), 4) == lax.div(in_row, 32))
        & (lax.rem(out_row, 4) == lax.rem(in_row, 4))
    )
    hits = one_hot(plan[...] == me)
    live_row = mm(jnp.ones((128, 32), BF16), hits).astype(BF16)
    live_col = mm_tn(hits, jnp.ones((32, 128), BF16)).astype(BF16)
    lane = iota((64, 256), 1)
    sender = lax.div(lax.rem(lane, 32), 4) * 8 + lax.div(lane, 32)
    order = iota((64, 256), 0)
    spot = mm(live_row, one_hot(order < sender)) * 4.0
    spot += lax.rem(iota((128, 256), 1), 4).astype(F32)
    spot = jnp.where(mm(live_row, one_hot(order == sender)) > 0.5, spot, -1.0)
    to_rows = one_hot(spot == iota((128, 256), 0).astype(F32))

    loads.pop(L_V).wait()
    loads.pop(L_DO).wait()
    send_do[...] = stage(dov)

    lens = lengths[...]
    high = lax.div(lens, 32)
    low = lens - high * 32
    upper = one_hot(iota((16, 16), 0) <= iota((16, 16), 1))
    ends = mm(high.astype(F32).astype(BF16), upper) * 32.0 + mm(low.astype(F32).astype(BF16), upper)
    mine = iota((8, 16), 0) == d
    end_row = jnp.sum(jnp.where(mine, ends, 0.0), axis=0, keepdims=True)
    len_row = jnp.sum(jnp.where(mine, lens.astype(F32), 0.0), axis=0, keepdims=True)
    position = (c * 128 + iota((128, 16), 0)).astype(F32)
    seq_start = jnp.sum(jnp.where(end_row <= position, len_row, 0.0), axis=1, keepdims=True)
    angle = (position[:, 0:1] - seq_start) * freq[...]
    cosine = jnp.cos(angle)
    sine = jnp.sin(angle)
    signed = jnp.where(iota((128, 128), 1) < 64, -sine, sine)

    arrived(PART)
    key_proj = (part_r[0] + part_r[1] + part_r[2] + part_r[3]).astype(BF16)
    zkv_s[...] = mm(to_slots, jnp.concatenate([key_proj, vv[...]], axis=1)).astype(BF16)

    def send_blocks(source, target, phase, size):
        def one(k, carry):
            g = far_first(k, 8)[0]
            remote(
                source.at[rows(g * size, size, size), :],
                target.at[rows(d * size, size, size), :],
                phase,
                (g, c, t),
            ).start()
            return carry

        lax.fori_loop(0, 7, one, 0)
        started(phase)
        target[rows(d * size, size, size), :] = source[rows(d * size, size, size), :]

    send_blocks(zkv_s, zkv_r, ZKV, 32)
    send_slots(send_q, recv_q, Q, 32, 63)
    started(Q)
    own_slot(send_q, recv_q)
    own_slot(send_do, recv_do)

    slot = lax.div(iota((64, 1024), 1), 16)
    col = iota((128, 1024), 1)
    spot = mm(live_row, one_hot(iota((64, 1024), 0) < slot)) * 4.0 + (
        lax.rem(col, 4) + 128 * lax.div(lax.rem(col, 16), 4)
    ).astype(F32)
    spot = jnp.where(mm(live_row, one_hot(iota((64, 1024), 0) == slot)) > 0.5, spot, -1.0)
    for ch in range(4):
        rmat[ch * 128 : ch * 128 + 128, :] = one_hot(
            spot == (iota((128, 1024), 0) + ch * 128).astype(F32)
        )

    arrived(ZKV)
    ckv_s[...] = mm(regroup, zkv_r[...]).astype(BF16)

    def send_ckv(k, carry):
        cc = lax.rem(c + k, 8)
        remote(
            ckv_s.at[rows(cc * 32, 32, 32), :], ckv_r.at[rows(c * 32, 32, 32), :], CKV, (d, cc, t)
        ).start()
        return carry

    lax.fori_loop(1, 8, send_ckv, 0)
    started(CKV)
    ckv_r[rows(c * 32, 32, 32), :] = ckv_s[rows(c * 32, 32, 32), :]
    send_slots(send_do, recv_do, DO, 0, 16)
    for k in range(8):

        @pl.when(k < c)
        def _():
            terms_r[k * 128 : k * 128 + 128, :] = jnp.zeros((128, 256), BF16)

    arrived(CKV)
    pair = mm(to_rows, ckv_r[...])
    raw = pair[:, 0:128]
    keys = raw * cosine + pltpu.roll(raw, 64, 1) * signed
    kv_all[rows(c * 128, 128, 128), 0:128] = keys.astype(BF16)
    kv_all[rows(c * 128, 128, 128), 128:256] = pair[:, 128:256].astype(BF16)

    def send_gather(k, carry):
        cc = lax.rem(c + k, 8)
        block = kv_all.at[rows(c * 128, 128, 128), :]
        remote(block, block, GATHER, (d, cc, t)).start()
        return carry

    lax.fori_loop(1, 8, send_gather, 0)
    started(GATHER)
    send_slots(send_do, recv_do, DO, 16, 63)
    started(DO)

    lax.fori_loop(3, 6, send_tokens, 0)
    back[...] = rmat[0:128, :].T
    collect[...] = smat[:, 0:128].T

    arrived(Q)
    heads = mm(rmat[...], recv_q[...]).astype(BF16)
    for ch in range(4):
        for k in range(2):
            qs[(2 * ch + k) * 128 : (2 * ch + k) * 128 + 128, :] = heads[
                ch * 128 : ch * 128 + 128, k * 128 : k * 128 + 128
            ]
    scale = HEAD**-0.5
    key_at = iota((1024, 128), 0).astype(F32)
    query_at = (c * 128 + iota((16, 128), 1)).astype(F32)
    end_all = jnp.where(mine, ends, 0.0)
    len_all = jnp.where(mine, lens.astype(F32), 0.0)
    pick = jnp.ones((8, 128), F32)
    end_col = lax.dot_general(
        end_all, pick, (((0,), (0,)), ((), ())),
        precision=lax.Precision.HIGHEST, preferred_element_type=F32,
    )
    len_col = lax.dot_general(
        len_all, pick, (((0,), (0,)), ((), ())),
        precision=lax.Precision.HIGHEST, preferred_element_type=F32,
    )
    starts = jnp.sum(jnp.where(end_col <= query_at, len_col, 0.0), axis=0, keepdims=True)
    hidden = jnp.where((key_at <= query_at[0:1]) & (key_at >= starts), 0.0, -1e30)

    arrived(GATHER)
    key_t[...] = kv_all[:, 0:128].T
    value_t[...] = kv_all[:, 128:256].T

    hidden = jnp.concatenate([hidden, hidden], axis=1)

    def forward(h, carry):
        here = rows(h * 256, 256, 256)
        scores = mm_nt(kv_all[:, 0:128], qs[here, :]) * (scale * LOG2E) + hidden
        grown = jnp.exp2(scores - jnp.max(scores, axis=0, keepdims=True))
        chance = grown * (1.0 / jnp.sum(grown, axis=0, keepdims=True))
        prob[:, here] = chance
        rounded = chance.astype(BF16)
        weights[:, here] = rounded
        out = mm(value_t[...], rounded).astype(BF16)
        att_t[:, here] = out
        for k in range(2):
            att[:, rows(h * 256 + k * 128, 128, 128)] = out[:, k * 128 : k * 128 + 128].T
        return carry

    lax.fori_loop(0, 4, forward, 0)
    stores[L_ATT] = local(att, att_h, L_ATT)
    stores[L_ATT].start()

    arrived(DO)
    heads = mm(rmat[...], recv_do[...]).astype(BF16)
    for ch in range(4):
        for k in range(2):
            low = (2 * ch + k) * 128
            block = heads[ch * 128 : ch * 128 + 128, k * 128 : k * 128 + 128]
            dos[low : low + 128, :] = block
            products = block.T.astype(F32) * att_t[:, low : low + 128].astype(F32)
            delta[:, low : low + 128] = jnp.sum(products, axis=0, keepdims=True)

    def backward(k, carry):
        chunk = lax.rem(lax.div(c, 2) + 1 + k, 4)
        here = rows(chunk * 256, 256, 256)
        grads = mm_nt(kv_all[here, 128:256], dos[...]) - delta[...]
        rounded = (prob[here, :] * grads).astype(BF16)
        dscores[here, :] = rounded
        terms_s[here, 0:128] = mm(rounded, qs[...]).astype(BF16)
        terms_s[here, 128:256] = mm(weights[here, :], dos[...]).astype(BF16)
        for part in range(2):
            owner = chunk * 2 + part

            @pl.when(owner < c)
            def _():
                term_copy(owner, None).start()

        return carry

    lax.fori_loop(0, 4, backward, 0)
    terms_r[rows(c * 128, 128, 128), :] = terms_s[rows(c * 128, 128, 128), :]

    def query_grads(h, carry):
        grad = (mm(key_t[...], dscores[:, rows(h * 256, 256, 256)]) * scale).astype(BF16)
        for k in range(2):
            qg[:, rows(h * 256 + k * 128, 128, 128)] = grad[:, k * 128 : k * 128 + 128].T
        return carry

    lax.fori_loop(0, 4, query_grads, 0)
    stores[L_QG] = local(qg, qg_h, L_QG)
    stores[L_QG].start()

    for k in range(8):

        @pl.when(k > c)
        def _():
            term_copy(k, k).wait_recv()

    owned = terms_r[0:128, :].astype(F32)
    for k in range(1, 8):
        owned += terms_r[k * 128 : k * 128 + 128, :].astype(F32)
    rot_grad = owned[:, 0:128] * scale
    key_grad = (rot_grad * cosine - pltpu.roll(rot_grad, 64, 1) * signed).astype(BF16)
    back_s[...] = mm(back[...], key_grad).astype(BF16)
    send_slots(back_s, back_r, BACK, 0, 63)
    started(BACK)
    own_slot(back_s, back_r)
    lax.fori_loop(6, 8, send_tokens, 0)
    started(TOK)
    vg[...] = owned[:, 128:256].astype(BF16)
    stores[L_VG] = local(vg, vg_h, L_VG)
    stores[L_VG].start()
    old, new_col = iota((128, 256), 0), iota((128, 256), 1)
    packed = (lax.div(lax.rem(old, 64), 32) == lax.div(new_col, 128)) & (
        lax.div(old, 64) * 32 + lax.rem(old, 32) == lax.rem(new_col, 64)
    )
    upper_rows = lax.rem(new_col, 128) < 64
    pack_a, pack_b = one_hot(packed & upper_rows), one_hot(packed & ~upper_rows)
    arrived(BACK)
    own_grads = mm(collect[...], back_r[...]).astype(BF16)

    moved = (mm(own_grads[0:64], pack_a) + mm(own_grads[64:128], pack_b)).astype(BF16)
    for k in range(2):
        kgs[k] = moved[:, k * 128 : k * 128 + 128]

    def send_grads(k, carry):
        cc = lax.rem(c + k, 8)
        tt = lax.rem(t + lax.div(k, 8), 4)
        remote(
            kgs.at[lax.div(cc, 4)],
            kgr.at[rows(c * 64, 64, 64), rows(t * 128, 128, 128)],
            KEYS,
            (d, cc, tt),
        ).start()
        return carry

    lax.fori_loop(1, 32, send_grads, 0)
    started(KEYS)
    kgr[rows(c * 64, 64, 64), rows(t * 128, 128, 128)] = kgs[x]
    fg_s[...] = own_grads

    def send_heads(k, carry):
        tt = lax.rem(t + k, 4)
        remote(fg_s, fg_r.at[:, rows(t * 128, 128, 128)], HEADS, (d, c, tt)).start()
        return carry

    lax.fori_loop(1, 4, send_heads, 0)
    started(HEADS)
    fg_r[:, rows(t * 128, 128, 128)] = own_grads
    arrived(TOK)
    arrived(KEYS)
    turned = kgr[...].T
    even = jnp.concatenate([turned[k * 128 : k * 128 + 64] for k in range(4)], axis=0)
    odd = jnp.concatenate([turned[k * 128 + 64 : k * 128 + 128] for k in range(4)], axis=0)
    part = mm(even, toks[0]) + mm(odd, toks[1])
    pieces = [part[:, k * 256 : k * 256 + 256].reshape(32, 1, 8, 256) for k in range(2)]
    sum_s[...] = jnp.concatenate(pieces, axis=1).reshape(512, 256).astype(BF16)

    def send_sums(k, carry):
        g, away = far_first(k, 4)
        yy = lax.rem(y + away, 4)
        remote(
            sum_s.at[rows((g * 4 + yy) * 16, 16, 16), :],
            sum_r.at[rows((d * 4 + y) * 16, 16, 16), :],
            ZSUM,
            (g, x * 4 + yy, t),
        ).start()
        return carry

    lax.fori_loop(0, 31, send_sums, 0)
    started(ZSUM)
    sum_r[rows((d * 4 + y) * 16, 16, 16), :] = sum_s[rows((d * 4 + y) * 16, 16, 16), :]
    arrived(HEADS)
    for k in range(4):
        fg[:, k * 512 : k * 512 + 512] = mm(
            fg_r[...], wv[:, k * 512 : k * 512 + 512]
        ).astype(BF16)
    stores[L_FG] = local(fg, fg_h, L_FG)
    stores[L_FG].start()
    arrived(ZSUM)
    added = sum_r[0:64, :].astype(F32)
    for k in range(1, 8):
        added += sum_r[k * 64 : k * 64 + 64, :].astype(F32)
    for k in range(8):
        kwg[:, k * 256 : k * 256 + 256] = added[k * 8 : k * 8 + 8]
    stores[L_KWG] = local(kwg, kwg_h, L_KWG)
    stores[L_KWG].start()
    for k in range(8):

        @pl.when(k < c)
        def _():
            term_copy(k, None).wait_send()

    finish()


def copy_out(*refs):
    sem = refs[15]
    reads = [pltpu.make_async_copy(refs[k], refs[10 + k], sem.at[0, k]) for k in range(5)]
    writes = [pltpu.make_async_copy(refs[10 + k], refs[5 + k], sem.at[1, k]) for k in range(5)]
    for item in reads:
        item.start()
    for read, write in zip(reads, writes):
        read.wait()
        write.start()
    for item in writes:
        item.wait()


def shards(tokens, queries, values, out_grad, key_weight, plan, lengths):
    half = np.arange(128) % 64
    freq = np.exp(-(half.astype(np.float32) * np.float32(2.0 / HEAD)) * np.float32(math.log(THETA)))
    freq = jnp.asarray(freq.astype(np.float32).reshape(1, 128))
    vmem = pl.BlockSpec(memory_space=pltpu.VMEM)
    hbm = pl.BlockSpec(memory_space=pl.ANY)
    scratch = [
        ((128, 2048), BF16), ((128, 1024), BF16), ((128, 128), BF16), ((128, 1024), BF16),
        ((512, 2048), BF16), ((1024, 512), BF16), ((512, 1024), BF16),
        ((1024, 256), BF16), ((1024, 256), BF16), ((1024, 256), BF16), ((1024, 256), BF16),
        ((256, 256), BF16), ((256, 256), BF16), ((256, 256), BF16), ((256, 256), BF16),
        ((4, 128, 128), F32), ((4, 128, 128), F32),
        ((1024, 256), BF16), ((128, 1024), BF16), ((128, 1024), BF16), ((1024, 128), BF16),
        ((1024, 128), BF16), ((1024, 1024), F32), ((1024, 1024), BF16), ((1024, 1024), BF16),
        ((128, 1024), BF16), ((128, 1024), BF16), ((1, 1024), F32), ((128, 1024), BF16),
        ((1024, 256), BF16), ((1024, 256), BF16), ((1024, 128), BF16),
        ((128, 1024), BF16), ((1024, 128), BF16), ((1024, 128), BF16), ((2, 64, 128), BF16),
        ((512, 512), BF16), ((2, 512, 512), BF16), ((512, 256), BF16), ((512, 256), BF16),
        ((128, 128), BF16), ((128, 512), BF16), ((128, 128), BF16), ((128, 2048), BF16),
        ((8, 2048), F32),
    ]
    shapes = (
        jax.ShapeDtypeStruct((128, 1024), BF16),
        jax.ShapeDtypeStruct((128, 1024), BF16),
        jax.ShapeDtypeStruct((128, 128), BF16),
        jax.ShapeDtypeStruct((128, 2048), BF16),
        jax.ShapeDtypeStruct((8, 2048), F32),
    )
    results = pl.pallas_call(
        kernel,
        out_shape=shapes,
        in_specs=[vmem] * 3 + [hbm] * 5,
        out_specs=(hbm,) * 5,
        scratch_shapes=[pltpu.VMEM(shape, dtype) for shape, dtype in scratch]
        + [
            pltpu.SemaphoreType.DMA((10,)),
            pltpu.SemaphoreType.DMA((PHASES,)),
            pltpu.SemaphoreType.DMA((PHASES,)),
            pltpu.SemaphoreType.DMA((2, 8)),
        ],
        compiler_params=pltpu.CompilerParams(
            collective_id=0, has_side_effects=True, vmem_limit_bytes=62 * 1024 * 1024
        ),
    )(plan.T, lengths, freq, tokens, queries, values, out_grad, key_weight)
    return pl.pallas_call(
        copy_out,
        out_shape=shapes,
        in_specs=[hbm] * 5,
        out_specs=(hbm,) * 5,
        scratch_shapes=[pltpu.VMEM(item.shape, item.dtype) for item in shapes]
        + [pltpu.SemaphoreType.DMA((2, 5))],
        compiler_params=pltpu.CompilerParams(vmem_limit_bytes=62 * 1024 * 1024),
    )(*results)


def solution(mesh):
    both = P(("dp", "ctx"), "tensor")
    return jax.shard_map(
        shards,
        mesh=mesh,
        in_specs=(both, both, both, both, P(None, "tensor"), P(), P()),
        out_specs=(both,) * 5,
        check_vma=False,
    )
```
